256 devices in a mesh: batch: 8 (over z), proto: 32 (over y, x, core).
Axes of the slice: x: 4, y: 4, z: 8, core: 2. Of those that a mesh axis runs over, the one named last changes fastest.
Arguments:
- student_features: bfloat16 [12288, 256], P('batch'), may hold values from -8 to 8, as said below
- teacher_features: bfloat16 [12288, 256], P('batch'), may hold values from -8 to 8, as said below
- student_protos: bfloat16 [256, 65536], P(None, 'proto'), may hold values from -2 to 2, as said below
- teacher_protos: bfloat16 [256, 65536], P(None, 'proto'), may hold values from -2 to 2
Outputs:
- feature_grads: float32 [12288, 256], P('batch')
- proto_grads: float32 [65536, 256], P('proto')
The draws below stay inside these ranges and needn't reach their ends.
Inputs may be any that keep to these rules, and one draw needn't show every extreme that they name: `student_features`: features of one crop; student and teacher features of a crop are related. `teacher_features`: features of one crop. `student_protos`: the teacher prototypes lie near the student ones.
All inputs are finite; a program needn't handle non-finite values.
Results may differ from the reference program's by a relative error of at most 0.0067.
Values sent between devices are 32-bit elements; how exact they have to be, the bound alone decides.
A program may use at most 128 MiB of HBM per device.

```python
import math
import jax
import jax.numpy as jnp
from jax import lax

D = 256
ITERS = 3
CROPS = 12288
PROTOS = 65536


def shared_direction(key):
    signs = jax.random.randint(jax.random.fold_in(key, 11), (D,), 0, 2)
    return (2.0 * signs.astype(jnp.float32) - 1.0) / math.sqrt(D)


def feature_bases(key):
    normal_part = jnp.clip(jax.random.normal(jax.random.fold_in(key, 21), (CROPS, D), jnp.float32), -4.0, 4.0)
    return normal_part


def proto_bases(key):
    normal_part = jnp.clip(jax.random.normal(jax.random.fold_in(key, 31), (D, PROTOS), jnp.float32), -4.0, 4.0)
    return normal_part


def feature_mix(base, direction, span):
    position = jnp.arange(CROPS).astype(jnp.float32) / CROPS
    strength = span * position
    return base + strength[:, None] * math.sqrt(D) * direction[None, :]


def proto_mix(base, direction, span):
    position = jnp.arange(PROTOS).astype(jnp.float32) / PROTOS
    strength = span * position
    return (base + strength[None, :] * math.sqrt(D) * direction[:, None]) / math.sqrt(D)


def draw_teacher_features(key, part):
    direction = shared_direction(key)
    normal_part = feature_bases(key)
    values = feature_mix(normal_part, direction, 0.6)
    return values.astype(jnp.bfloat16)


def draw_student_features(key, part):
    direction = shared_direction(key)
    normal_part = feature_bases(key)
    key = jax.random.fold_in(key, 2)
    own = jnp.clip(jax.random.normal(key, (CROPS, D), jnp.float32), -4.0, 4.0)
    values = feature_mix(normal_part + 0.7 * own, direction, 0.6)
    return values.astype(jnp.bfloat16)


def draw_teacher_protos(key, part):
    direction = shared_direction(key)
    normal_part = proto_bases(key)
    values = proto_mix(normal_part, direction, 0.4)
    return values.astype(jnp.bfloat16)


def draw_student_protos(key, part):
    direction = shared_direction(key)
    normal_part = proto_bases(key)
    key = jax.random.fold_in(key, 4)
    own = jnp.clip(jax.random.normal(key, (D, PROTOS), jnp.float32), -4.0, 4.0)
    values = proto_mix(normal_part + 0.5 * own, direction, 0.4)
    return values.astype(jnp.bfloat16)


def setup_inputs(seed: int = 0) -> dict:
    key_of = jax.random.split(jax.random.key(seed), 5)
    student_features = draw_student_features(jax.random.fold_in(key_of[4], 71), 0)
    teacher_features = draw_teacher_features(jax.random.fold_in(key_of[4], 71), 0)
    student_protos = draw_student_protos(jax.random.fold_in(key_of[4], 71), 0)
    teacher_protos = draw_teacher_protos(jax.random.fold_in(key_of[4], 71), 0)
    return {"student_features": student_features, "teacher_features": teacher_features, "student_protos": student_protos, "teacher_protos": teacher_protos}


teacher_temp = 0.04
student_temp = 0.1
loss_scale = 4096.0
epsilon = 1e-06

def unit_rows(values):
    floats = values.astype(jnp.float32)
    length = jnp.sqrt(lax.optimization_barrier(jnp.sum(floats * floats, axis=1, keepdims=True)) + epsilon)
    return (floats / length, length)

def project_back(grads, unit, length):
    return (grads - unit * lax.optimization_barrier(jnp.sum(unit * grads, axis=1, keepdims=True))) / length

def reference(student_features, teacher_features, student_protos, teacher_protos):
    student_unit, student_len = unit_rows(student_features)
    teacher_unit, _ = unit_rows(teacher_features)
    proto_unit, proto_len = unit_rows(student_protos.T)
    anchor_unit, _ = unit_rows(teacher_protos.T)
    student_half = student_unit.astype(jnp.bfloat16)
    teacher_half = teacher_unit.astype(jnp.bfloat16)
    proto_half = proto_unit.astype(jnp.bfloat16)
    anchor_half = anchor_unit.astype(jnp.bfloat16)
    contract_last = (((1,), (1,)), ((), ()))
    contract_first = (((0,), (0,)), ((), ()))
    block_size = math.gcd(CROPS, 256)
    blocks = CROPS // block_size
    teacher_blocks = teacher_half.reshape(blocks, block_size, D)
    student_blocks = student_half.reshape(blocks, block_size, D)

    def exp_block(crop_rows):
        return jnp.exp(lax.dot_general(crop_rows, anchor_half, contract_last, preferred_element_type=jnp.float32) / teacher_temp)

    def first_pass(total, crop_rows):
        return (total + lax.optimization_barrier(jnp.sum(exp_block(crop_rows), axis=0)), None)
    column_total, _ = lax.scan(first_pass, jnp.zeros((PROTOS,), jnp.float32), teacher_blocks)
    col_scale = 1.0 / column_total
    for sweep in range(ITERS - 1):

        def middle_pass(total, crop_rows, scale=col_scale):
            weights = exp_block(crop_rows)
            row_scale = 1.0 / jnp.dot(weights, scale, precision=lax.Precision.HIGHEST)
            return (total + jnp.dot(row_scale, weights, precision=lax.Precision.HIGHEST), None)
        column_total, _ = lax.scan(middle_pass, jnp.zeros((PROTOS,), jnp.float32), teacher_blocks)
        col_scale = 1.0 / column_total

    def last_pass(total, paired):
        teacher_rows, student_rows = paired
        weights = exp_block(teacher_rows)
        row_scale = 1.0 / jnp.dot(weights, col_scale, precision=lax.Precision.HIGHEST)
        targets = row_scale[:, None] * weights * col_scale[None, :]
        student_exp = jnp.exp(lax.dot_general(student_rows, proto_half, contract_last, preferred_element_type=jnp.float32) / student_temp)
        predicted = student_exp / lax.optimization_barrier(jnp.sum(student_exp, axis=1, keepdims=True))
        grad_logits = (loss_scale * (predicted - targets) / student_temp).astype(jnp.bfloat16)
        feature_terms = jnp.dot(grad_logits, proto_half, preferred_element_type=jnp.float32)
        total = total + lax.dot_general(grad_logits, student_rows, contract_first, preferred_element_type=jnp.float32)
        return (total, feature_terms)
    proto_terms, feature_blocks = lax.scan(last_pass, jnp.zeros((PROTOS, D), jnp.float32), (teacher_blocks, student_blocks))
    feature_terms = feature_blocks.reshape(CROPS, D)
    feature_grads = project_back(feature_terms, student_unit, student_len)
    proto_grads = project_back(proto_terms, proto_unit, proto_len)
    return (feature_grads, proto_grads)
```

```python
import jax
import jax.numpy as jnp
from jax import lax
from jax.experimental import pallas as pl
from jax.experimental.pallas import tpu as pltpu
from jax.sharding import PartitionSpec as P

MESH = pl.DeviceIdType.MESH
F32 = jnp.float32
BF16 = jnp.bfloat16

epsilon = 1e-06
teacher_rate = 25.0
student_rate = 10.0
grad_scale = 40960.0

CROPS = 1536
PROTOS = 2048
D = 256
Z = 8
CHIPS = 16
OWN = PROTOS // Z
SUB = OWN // 4
HALF = CROPS // 2
PIECE = HALF // CHIPS


def rows_at(start, size, step):
    return pl.ds(pl.multiple_of(start, step), size)


def normalise_rows(src, dst):
    def body(i, carry):
        rows = rows_at(i * 256, 256, 256)
        floats = src[rows, :].astype(F32)
        length = jnp.sqrt(jnp.sum(floats * floats, axis=1, keepdims=True) + epsilon)
        dst[rows, :] = (floats / length).astype(BF16)
        return carry

    lax.fori_loop(0, CROPS // 256, body, 0)


def normalise_columns(src, dst, dst_t):
    def body(i, carry):
        cols = rows_at(i * 256, 256, 256)
        floats = src[:, cols].astype(F32)
        length = jnp.sqrt(jnp.sum(floats * floats, axis=0, keepdims=True) + epsilon)
        unit = floats / length
        dst[:, cols] = unit.astype(BF16)
        dst_t[cols, :] = unit.T.astype(BF16)
        return carry

    lax.fori_loop(0, PROTOS // 256, body, 0)


def exp_tiles(rows_ref, cols_ref, out, rate, transposed):
    count, width = out.shape
    dims = (((1,), (1,)), ((), ())) if transposed else (((1,), (0,)), ((), ()))

    def body(i, total):
        rows = rows_at(i * 256, 256, 256)
        logits = lax.dot_general(rows_ref[rows, :], cols_ref[...], dims, preferred_element_type=F32)
        values = jnp.exp(logits * rate)
        out[rows, :] = values.astype(BF16)
        return total + jnp.sum(values.reshape(32, 8, width), axis=0)

    total = lax.fori_loop(0, count // 256, body, jnp.zeros((8, width), F32))
    return jnp.sum(total, axis=0, keepdims=True)


def vector_times(vector, matrix):
    high = vector.astype(BF16).astype(F32)
    low = vector - high
    row = lax.broadcasted_iota(jnp.int32, (16, vector.shape[1]), 0)
    left = jnp.where(row == 0, high, jnp.where(row == 1, low, 0.0)).astype(BF16)
    return jnp.sum(jnp.dot(left, matrix[...], preferred_element_type=F32), axis=0, keepdims=True)


def to_rows(vector, dst):
    for i in range(vector.shape[1] // 128):
        part = vector[:, i * 128 : (i + 1) * 128]
        dst[i * 128 : (i + 1) * 128, :] = jnp.broadcast_to(part, (128, 128)).T


def wide(narrow):
    return jnp.concatenate([narrow, narrow], axis=1)


def kernel(
    sf, tf, sp, tp, fg_out, pg_out,
    E, ET, S, ST, sh, th, ph, phT, ah, ahT,
    scaled_s, scaled_p, row_scale, col_scale, a_scale,
    F1, F2, P1,
    col_src, col_recv, row_part, row_sib, row_src, row_recv,
    own, snd_r, snd_l, rcv_r, rcv_l, pg,
    f_sib, f_recv, fg,
    col_s, col_r, rc_s, rc_r, rp_s, rp_r,
    rsr_s, rsr_r, rsl_s, rsl_r, agr_s, agr_r, agl_s, agl_r,
    fc_s, fc_r, fx_s, fx_r, fa_s, fa_r, ff_s, ff_r, po_s, fo_s,
):
    z = lax.axis_index("batch")
    p = lax.axis_index("proto")
    core = lax.rem(p, 2)
    chip = p // 2
    sibling = (z, chip * 2 + 1 - core)
    right = (lax.rem(z + 1, Z), p)
    left = (lax.rem(z + Z - 1, Z), p)

    def same_core(d):
        return (z, lax.rem(chip + d, CHIPS) * 2 + core)

    barrier = pltpu.get_barrier_semaphore()

    def greet_z(d, carry):
        pl.semaphore_signal(barrier, inc=1, device_id=(lax.rem(z + d, Z), p), device_id_type=MESH)
        return carry

    lax.fori_loop(1, Z, greet_z, 0)

    def greet_plane(d, carry):
        pl.semaphore_signal(barrier, inc=1, device_id=same_core(d), device_id_type=MESH)
        return carry

    lax.fori_loop(1, CHIPS, greet_plane, 0)
    pl.semaphore_signal(barrier, inc=1, device_id=sibling, device_id_type=MESH)

    def remote(src, dst, ss, rs, target):
        return pltpu.make_async_remote_copy(
            src_ref=src, dst_ref=dst, send_sem=ss, recv_sem=rs, device_id=target, device_id_type=MESH
        )

    def col_copy(i, d):
        return remote(
            col_src.at[i], col_recv.at[i, d - 1], col_s.at[i, d - 1], col_r.at[i, d - 1],
            (lax.rem(z + d, Z), p),
        )

    def col_send(i, partial):
        col_src[i] = partial
        for d in (4, 3, 5, 2, 6, 1, 7):
            col_copy(i, d).start()

    def col_total(i):
        for d in (1, 7, 2, 6, 3, 5, 4):
            col_copy(i, d).wait_recv()
        return col_src[i] + jnp.sum(col_recv[i], axis=0)

    def pair_copy(i):
        return remote(row_part.at[i], row_sib.at[i], rc_s.at[i], rc_r.at[i], sibling)

    def chip_copy(i, d):
        return remote(
            row_src.at[i], row_recv.at[i, d - 1], rp_s.at[i, d - 1], rp_r.at[i, d - 1], same_core(d)
        )

    def row_send(i, partial):
        row_part[i] = partial
        pair_copy(i).start()
        pair_copy(i).wait_recv()
        row_src[i] = row_part[i] + row_sib[i]
        for d in range(1, CHIPS):
            chip_copy(i, d).start()

    def row_total(i):
        for d in range(1, CHIPS):
            chip_copy(i, d).wait_recv()
        return row_src[i] + jnp.sum(row_recv[i], axis=0)

    normalise_rows(tf, th)
    normalise_columns(tp, ah, ahT)
    partial = exp_tiles(th, ah, E, teacher_rate, False)
    pl.semaphore_wait(barrier, Z - 1 + CHIPS - 1 + 1)

    col_send(0, partial)
    exp_tiles(ahT, th, ET, teacher_rate, True)
    scale = 1.0 / col_total(0)

    row_send(0, vector_times(scale, ET))
    normalise_rows(sf, sh)
    normalise_columns(sp, ph, phT)
    student_partial = exp_tiles(phT, sh, ST, student_rate, True)
    scale = 1.0 / row_total(0)

    col_send(1, vector_times(scale, E))
    row_send(3, student_partial)
    exp_tiles(sh, ph, S, student_rate, False)
    scale = 1.0 / col_total(1)

    row_send(1, vector_times(scale, ET))

    def student_features(i, carry):
        rows = rows_at(i * 256, 256, 256)
        F1[rows, :] = jnp.dot(S[rows, :], phT[...], preferred_element_type=F32)
        return carry

    lax.fori_loop(0, CROPS // 256, student_features, 0)
    scale = 1.0 / row_total(1)

    col_send(2, vector_times(scale, E))
    to_rows(grad_scale / row_total(3), a_scale)
    scaled_s[...] = (sh[...].astype(F32) * wide(a_scale[...])).astype(BF16)

    def student_protos(i, carry):
        rows = rows_at(i * 256, 256, 256)
        P1[rows, :] = jnp.dot(ST[rows, :], scaled_s[...], preferred_element_type=F32)
        return carry

    lax.fori_loop(0, PROTOS // 256, student_protos, 0)
    scale = 1.0 / col_total(2)

    row_send(2, vector_times(scale, ET))
    to_rows(scale, col_scale)
    scaled_p[...] = (phT[...].astype(F32) * wide(col_scale[...])).astype(BF16)

    def teacher_features(i, carry):
        rows = rows_at(i * 256, 256, 256)
        F2[rows, :] = jnp.dot(E[rows, :], scaled_p[...], preferred_element_type=F32)
        return carry

    lax.fori_loop(0, CROPS // 256, teacher_features, 0)
    to_rows(grad_scale / row_total(2), row_scale)
    scaled_s[...] = (sh[...].astype(F32) * wide(row_scale[...])).astype(BF16)

    def chunk(index):
        rows = rows_at(index * OWN, OWN, OWN)
        product = jnp.dot(ET[rows, :], scaled_s[...], preferred_element_type=F32)
        return P1[rows, :] - wide(col_scale[rows, :]) * product

    def ahead(d):
        return lax.rem(z + d, Z)

    def part(values, j):
        return values[j * SUB : (j + 1) * SUB, :]

    def rs_r(d, j):
        return remote(snd_r.at[d - 1, j], rcv_r.at[d - 1, j], rsr_s.at[d - 1, j], rsr_r.at[d - 1, j], right)

    def rs_l(d, j):
        return remote(snd_l.at[d - 1, j], rcv_l.at[d - 1, j], rsl_s.at[d - 1, j], rsl_r.at[d - 1, j], left)

    values = chunk(ahead(4))
    for j in (0, 1):
        snd_r[3, j] = part(values, j)
        rs_r(4, j).start()
    for j in (2, 3):
        snd_l[3, j] = part(values, j)
        rs_l(4, j).start()
    values = chunk(ahead(3))
    for j in (2, 3):
        snd_r[2, j] = part(values, j)
        rs_r(3, j).start()
    for j in (0, 1):
        snd_r[2, j] = part(values, j)
    values = chunk(ahead(Z - 3))
    for j in (0, 1):
        snd_l[2, j] = part(values, j)
        rs_l(3, j).start()
    for j in (2, 3):
        snd_l[2, j] = part(values, j)

    F1[...] = F1[...] * wide(a_scale[...]) - F2[...] * wide(row_scale[...])
    feature_pair = remote(F1.at[rows_at((1 - core) * HALF, HALF, HALF)], f_sib, fc_s, fc_r, sibling)
    feature_pair.start()

    for d in (2, 1):
        values = chunk(ahead(d))
        for j in range(4):
            snd_r[d - 1, j] = part(values, j)
        values = chunk(ahead(Z - d))
        for j in range(4):
            snd_l[d - 1, j] = part(values, j)
    values = chunk(z)
    for j in range(4):
        own[j] = part(values, j)

    def pass_on(d, j_right, j_left):
        for j in j_right:
            rs_r(d + 1, j).wait_recv()
            snd_r[d - 1, j] = snd_r[d - 1, j] + rcv_r[d, j]
            rs_r(d, j).start()
        for j in j_left:
            rs_l(d + 1, j).wait_recv()
            snd_l[d - 1, j] = snd_l[d - 1, j] + rcv_l[d, j]
            rs_l(d, j).start()

    pass_on(3, (0, 1), (2, 3))
    pass_on(2, (2, 3), (0, 1))

    feature_pair.wait_recv()
    mine = rows_at(core * HALF, HALF, HALF)
    F2[mine, :] = F1[mine, :] + f_sib[...]

    def piece(c):
        return rows_at(core * HALF + c * PIECE, PIECE, PIECE)

    def piece_copy(d):
        return remote(
            F2.at[piece(lax.rem(chip + d, CHIPS))], f_recv.at[d - 1], fx_s.at[d - 1], fx_r.at[d - 1],
            same_core(d),
        )

    for d in range(1, CHIPS):
        piece_copy(d).start()

    pass_on(2, (0, 1), (2, 3))
    pass_on(1, (2, 3), (0, 1))
    pass_on(1, (0, 1), (2, 3))

    def ag_r(d, j):
        block = pg.at[rows_at(lax.rem(z + Z - (d - 1), Z) * OWN + j * SUB, SUB, SUB)]
        return remote(block, block, agr_s.at[d - 1, j], agr_r.at[d - 1, j], right)

    def ag_l(d, j):
        block = pg.at[rows_at(lax.rem(z + (d - 1), Z) * OWN + j * SUB, SUB, SUB)]
        return remote(block, block, agl_s.at[d - 1, j], agl_r.at[d - 1, j], left)

    def finish(j):
        rows = rows_at(z * OWN + j * SUB, SUB, SUB)
        terms = own[j] + rcv_r[0, j] + rcv_l[0, j]
        floats = sp[:, rows_at(z * OWN, OWN, OWN)].astype(F32).T[j * SUB : (j + 1) * SUB, :]
        length = jnp.sqrt(jnp.sum(floats * floats, axis=1, keepdims=True) + epsilon)
        unit = floats / length
        pg[rows, :] = (terms - unit * jnp.sum(unit * terms, axis=1, keepdims=True)) / length
        ag_r(1, j).start()
        ag_l(1, j).start()

    for j in (2, 3):
        rs_r(1, j).wait_recv()
    for j in (0, 1):
        rs_l(1, j).wait_recv()
    for j in (0, 1):
        rs_r(1, j).wait_recv()
        finish(j)
    for j in (2, 3):
        rs_l(1, j).wait_recv()
        finish(j)

    def out_copy(owner):
        rows = rows_at(owner * OWN, OWN, OWN)
        return pltpu.make_async_copy(pg.at[rows], pg_out.at[rows], po_s.at[owner])

    for d in range(1, CHIPS):
        piece_copy(d).wait_recv()
    my_piece = piece(chip)
    terms = F2[my_piece, :] + jnp.sum(f_recv[...], axis=0)
    floats = sf[my_piece, :].astype(F32)
    length = jnp.sqrt(jnp.sum(floats * floats, axis=1, keepdims=True) + epsilon)
    unit = floats / length
    fg[my_piece, :] = (terms - unit * jnp.sum(unit * terms, axis=1, keepdims=True)) / length

    def spread_copy(d):
        return remote(fg.at[my_piece], fg.at[my_piece], fa_s.at[d - 1], fa_r.at[d - 1], same_core(d))

    def arrived_copy(d):
        block = fg.at[piece(lax.rem(chip + CHIPS - d, CHIPS))]
        return remote(block, block, fa_s.at[d - 1], fa_r.at[d - 1], same_core(d))

    def hand_copy(d):
        block = fg.at[piece(lax.rem(chip + CHIPS - d, CHIPS))]
        return remote(block, block, ff_s.at[d], ff_r.at[d], sibling)

    def hand_arrived(d):
        start = (1 - core) * HALF + lax.rem(chip + CHIPS - d, CHIPS) * PIECE
        block = fg.at[rows_at(start, PIECE, PIECE)]
        return remote(block, block, ff_s.at[d], ff_r.at[d], sibling)

    for d in range(1, CHIPS):
        spread_copy(d).start()
    hand_copy(0).start()

    def arrived_r(d, j):
        block = pg.at[rows_at(lax.rem(z + Z - d, Z) * OWN + j * SUB, SUB, SUB)]
        return remote(block, block, agr_s.at[d - 1, j], agr_r.at[d - 1, j], right)

    def arrived_l(d, j):
        block = pg.at[rows_at(lax.rem(z + d, Z) * OWN + j * SUB, SUB, SUB)]
        return remote(block, block, agl_s.at[d - 1, j], agl_r.at[d - 1, j], left)

    out_copy(z).start()
    for d in (1, 2):
        for j in range(4):
            arrived_r(d, j).wait_recv()
            ag_r(d + 1, j).start()
            arrived_l(d, j).wait_recv()
            ag_l(d + 1, j).start()
        out_copy(lax.rem(z + Z - d, Z)).start()
        out_copy(lax.rem(z + d, Z)).start()
    for j in (0, 1):
        arrived_r(3, j).wait_recv()
        ag_r(4, j).start()
        arrived_l(3, j).wait_recv()
    for j in (2, 3):
        arrived_l(3, j).wait_recv()
        ag_l(4, j).start()
        arrived_r(3, j).wait_recv()
    out_copy(lax.rem(z + Z - 3, Z)).start()
    out_copy(lax.rem(z + 3, Z)).start()

    for d in range(1, CHIPS):
        arrived_copy(d).wait_recv()
        hand_copy(d).start()

    for j in (0, 1):
        arrived_r(4, j).wait_recv()
    for j in (2, 3):
        arrived_l(4, j).wait_recv()
    out_copy(lax.rem(z + 4, Z)).start()

    for d in range(CHIPS):
        hand_arrived(d).wait_recv()
    feature_out = pltpu.make_async_copy(fg, fg_out, fo_s)
    feature_out.start()

    for i in range(3):
        for d in range(1, Z):
            col_copy(i, d).wait_send()
    for i in range(4):
        pair_copy(i).wait_send()
        for d in range(1, CHIPS):
            chip_copy(i, d).wait_send()
    for d in (4, 3, 2, 1):
        for j in range(4):
            if d < 4 or j in (0, 1):
                rs_r(d, j).wait_send()
                ag_r(d, j).wait_send()
            if d < 4 or j in (2, 3):
                rs_l(d, j).wait_send()
                ag_l(d, j).wait_send()
    feature_pair.wait_send()
    for d in range(1, CHIPS):
        piece_copy(d).wait_send()
        spread_copy(d).wait_send()
    for d in range(CHIPS):
        hand_copy(d).wait_send()
    for owner in range(Z):
        out_copy(owner).wait()
    feature_out.wait()


def on_device(student_features, teacher_features, student_protos, teacher_protos):
    vmem = pltpu.VMEM
    dma = pltpu.SemaphoreType.DMA
    return pl.pallas_call(
        kernel,
        out_shape=(
            jax.ShapeDtypeStruct((CROPS, D), F32),
            jax.ShapeDtypeStruct((PROTOS, D), F32),
        ),
        in_specs=[pl.BlockSpec(memory_space=pltpu.VMEM)] * 4,
        out_specs=[pl.BlockSpec(memory_space=pl.ANY)] * 2,
        scratch_shapes=[
            vmem((CROPS, PROTOS), BF16),
            vmem((PROTOS, CROPS), BF16),
            vmem((CROPS, PROTOS), BF16),
            vmem((PROTOS, CROPS), BF16),
            vmem((CROPS, D), BF16),
            vmem((CROPS, D), BF16),
            vmem((D, PROTOS), BF16),
            vmem((PROTOS, D), BF16),
            vmem((D, PROTOS), BF16),
            vmem((PROTOS, D), BF16),
            vmem((CROPS, D), BF16),
            vmem((PROTOS, D), BF16),
            vmem((CROPS, 128), F32),
            vmem((PROTOS, 128), F32),
            vmem((CROPS, 128), F32),
            vmem((CROPS, D), F32),
            vmem((CROPS, D), F32),
            vmem((PROTOS, D), F32),
            vmem((3, 1, PROTOS), F32),
            vmem((3, Z - 1, 1, PROTOS), F32),
            vmem((4, 1, CROPS), F32),
            vmem((4, 1, CROPS), F32),
            vmem((4, 1, CROPS), F32),
            vmem((4, CHIPS - 1, 1, CROPS), F32),
            vmem((4, SUB, D), F32),
            vmem((4, 4, SUB, D), F32),
            vmem((4, 4, SUB, D), F32),
            vmem((4, 4, SUB, D), F32),
            vmem((4, 4, SUB, D), F32),
            vmem((PROTOS, D), F32),
            vmem((HALF, D), F32),
            vmem((CHIPS - 1, PIECE, D), F32),
            vmem((CROPS, D), F32),
            dma((3, Z - 1)),
            dma((3, Z - 1)),
            dma((4,)),
            dma((4,)),
            dma((4, CHIPS - 1)),
            dma((4, CHIPS - 1)),
        ]
        + [dma((4, 4))] * 8
        + [
            dma,
            dma,
            dma((CHIPS - 1,)),
            dma((CHIPS - 1,)),
            dma((CHIPS - 1,)),
            dma((CHIPS - 1,)),
            dma((CHIPS,)),
            dma((CHIPS,)),
            dma((Z,)),
            dma,
        ],
        compiler_params=pltpu.CompilerParams(
            collective_id=0, has_side_effects=True, vmem_limit_bytes=60 * 2**20
        ),
    )(student_features, teacher_features, student_protos, teacher_protos)


def solution(mesh):
    return jax.shard_map(
        on_device,
        mesh=mesh,
        in_specs=(P("batch", None), P("batch", None), P(None, "proto"), P(None, "proto")),
        out_specs=(P("batch", None), P("proto", None)),
        check_vma=False,
    )
```

```python
import jax
import jax.numpy as jnp
from jax import lax
from jax.experimental import pallas as pl
from jax.experimental.pallas import tpu as pltpu
from jax.sharding import PartitionSpec as P

MESH = pl.DeviceIdType.MESH
F32 = jnp.float32
BF16 = jnp.bfloat16

epsilon = 1e-06
log2_e = 1.4426950408889634
teacher_rate = 25.0 * log2_e
student_rate = 10.0 * log2_e
grad_scale = 40960.0

CROPS = 1536
PROTOS = 2048
D = 256
Z = 8
CHIPS = 16
OWN = PROTOS // Z
SUB = OWN // 4
HALF = CROPS // 2
PIECE = HALF // CHIPS


def rows_at(start, size, step):
    return pl.ds(pl.multiple_of(start, step), size)


def normalise_rows(src, dst):
    def body(i, carry):
        rows = rows_at(i * 256, 256, 256)
        floats = src[rows, :].astype(F32)
        length = jnp.sqrt(jnp.sum(floats * floats, axis=1, keepdims=True) + epsilon)
        dst[rows, :] = (floats / length).astype(BF16)
        return carry

    lax.fori_loop(0, CROPS // 256, body, 0)


def normalise_columns(src, dst):
    def body(i, carry):
        cols = rows_at(i * 256, 256, 256)
        floats = src[:, cols].astype(F32)
        length = jnp.sqrt(jnp.sum(floats * floats, axis=0, keepdims=True) + epsilon)
        dst[:, cols] = (floats / length).astype(BF16)
        return carry

    lax.fori_loop(0, PROTOS // 256, body, 0)


def transpose_into(src, dst):
    def body(i, carry):
        cols = rows_at(i * 256, 256, 256)
        dst[cols, :] = src[:, cols].astype(F32).T.astype(BF16)
        return carry

    lax.fori_loop(0, PROTOS // 256, body, 0)


def exp_tiles(rows_ref, cols_ref, out, rate, transposed):
    count, width = out.shape
    block = count // 2
    dims = (((1,), (1,)), ((), ())) if transposed else (((1,), (0,)), ((), ()))

    def body(i, total):
        rows = rows_at(i * block, block, block)
        logits = lax.dot_general(rows_ref[rows, :], cols_ref[...], dims, preferred_element_type=F32)
        values = jnp.exp2(logits * rate)
        out[rows, :] = values.astype(BF16)
        return total + jnp.sum(values.reshape(block // 8, 8, width), axis=0)

    total = lax.fori_loop(0, 2, body, jnp.zeros((8, width), F32))
    return jnp.sum(total, axis=0, keepdims=True)


def vector_times(vector, matrix):
    high = vector.astype(BF16).astype(F32)
    low = vector - high
    row = lax.broadcasted_iota(jnp.int32, (16, vector.shape[1]), 0)
    left = jnp.where(row == 0, high, jnp.where(row == 1, low, 0.0)).astype(BF16)
    return jnp.sum(jnp.dot(left, matrix[...], preferred_element_type=F32), axis=0, keepdims=True)


def to_rows(vector, dst):
    for i in range(vector.shape[1] // 128):
        part = vector[:, i * 128 : (i + 1) * 128]
        dst[i * 128 : (i + 1) * 128, :] = jnp.broadcast_to(part, (128, 128)).T


def wide(narrow):
    return jnp.concatenate([narrow, narrow], axis=1)


def scale_rows(values, scale, dst):
    dst[...] = (values[...].astype(F32) * wide(scale[...])).astype(BF16)


def products(matrix, columns, dst):
    block = dst.shape[0] // 2

    def body(i, carry):
        rows = rows_at(i * block, block, block)
        dst[rows, :] = jnp.dot(matrix[rows, :], columns[...], preferred_element_type=F32)
        return carry

    lax.fori_loop(0, 2, body, 0)


def kernel(
    sf_in, tf_in, sp_in, tp_in, fg, pg, sf, tf, sp, tp,
    E, ET, S, ST, sh, th, ph, phT, ah, ahT,
    scaled_s, scaled_p, row_scale, col_scale, a_scale,
    F1, F2, P1,
    col_src, col_recv, row_part, row_sib, row_src, row_recv,
    own, snd_r, snd_l, rcv_r, rcv_l, own_unit, own_len,
    f_sib, f_recv, in_s,
    col_s, col_r, rc_s, rc_r, rp_s, rp_r,
    rsr_s, rsr_r, rsl_s, rsl_r, agr_s, agr_r, agl_s, agl_r,
    fc_s, fc_r, fx_s, fx_r, fa_s, fa_r, ff_s, ff_r,
):
    z = lax.axis_index("batch")
    p = lax.axis_index("proto")
    core = lax.rem(p, 2)
    chip = p // 2
    sibling = (z, chip * 2 + 1 - core)
    right = (lax.rem(z + 1, Z), p)
    left = (lax.rem(z + Z - 1, Z), p)

    def same_core(d):
        return (z, lax.rem(chip + d, CHIPS) * 2 + core)

    barrier = pltpu.get_barrier_semaphore()

    def greet_z(d, carry):
        pl.semaphore_signal(barrier, inc=1, device_id=(lax.rem(z + d, Z), p), device_id_type=MESH)
        return carry

    lax.fori_loop(1, Z, greet_z, 0)

    def greet_plane(d, carry):
        pl.semaphore_signal(barrier, inc=1, device_id=same_core(d), device_id_type=MESH)
        return carry

    lax.fori_loop(1, CHIPS, greet_plane, 0)
    pl.semaphore_signal(barrier, inc=1, device_id=sibling, device_id_type=MESH)

    def load(i):
        src = (tf_in, tp_in, sf_in, sp_in)[i]
        dst = (tf, tp, sf, sp)[i]
        return pltpu.make_async_copy(src, dst, in_s.at[i])

    for i in range(4):
        load(i).start()

    def remote(src, dst, ss, rs, target):
        return pltpu.make_async_remote_copy(
            src_ref=src, dst_ref=dst, send_sem=ss, recv_sem=rs, device_id=target, device_id_type=MESH
        )

    def col_copy(i, d):
        return remote(
            col_src.at[i], col_recv.at[i, d - 1], col_s.at[i, d - 1], col_r.at[i, d - 1],
            (lax.rem(z + d, Z), p),
        )

    def col_send(i, partial):
        col_src[i] = partial
        for d in (4, 3, 5, 2, 6, 1, 7):
            col_copy(i, d).start()

    def col_total(i):
        for d in (1, 7, 2, 6, 3, 5, 4):
            col_copy(i, d).wait_recv()
        return col_src[i] + jnp.sum(col_recv[i], axis=0)

    def pair_copy(i):
        return remote(row_part.at[i], row_sib.at[i], rc_s.at[i], rc_r.at[i], sibling)

    def chip_copy(i, d):
        return remote(
            row_src.at[i], row_recv.at[i, d - 1], rp_s.at[i, d - 1], rp_r.at[i, d - 1], same_core(d)
        )

    def row_send(i, partial):
        row_part[i] = partial
        pair_copy(i).start()
        pair_copy(i).wait_recv()
        row_src[i] = row_part[i] + row_sib[i]
        for d in range(1, CHIPS):
            chip_copy(i, d).start()

    def row_total(i):
        for d in range(1, CHIPS):
            chip_copy(i, d).wait_recv()
        return row_src[i] + jnp.sum(row_recv[i], axis=0)

    load(0).wait()
    normalise_rows(tf, th)
    load(1).wait()
    normalise_columns(tp, ah)
    partial = exp_tiles(th, ah, E, teacher_rate, False)
    pl.semaphore_wait(barrier, Z - 1 + CHIPS - 1 + 1)

    col_send(0, partial)
    transpose_into(ah, ahT)
    exp_tiles(ahT, th, ET, teacher_rate, True)
    scale = 1.0 / col_total(0)

    row_send(0, vector_times(scale, ET))
    load(2).wait()
    normalise_rows(sf, sh)
    load(3).wait()
    normalise_columns(sp, ph)
    transpose_into(ph, phT)
    floats = sp[:, rows_at(z * OWN, OWN, OWN)].astype(F32).T
    length = jnp.sqrt(jnp.sum(floats * floats, axis=1, keepdims=True) + epsilon)
    own_len[...] = jnp.broadcast_to(length, (OWN, 128))
    own_unit[...] = floats / length
    scale = 1.0 / row_total(0)

    col_send(1, vector_times(scale, E))
    student_partial = exp_tiles(phT, sh, ST, student_rate, True)
    exp_tiles(sh, ph, S, student_rate, False)
    scale = 1.0 / col_total(1)

    row_send(1, vector_times(scale, ET))
    row_send(3, student_partial)
    products(S, phT, F1)
    scale = 1.0 / row_total(1)

    col_send(2, vector_times(scale, E))
    to_rows(grad_scale / row_total(3), a_scale)
    scale_rows(sh, a_scale, scaled_s)
    products(ST, scaled_s, P1)
    scale = 1.0 / col_total(2)

    row_send(2, vector_times(scale, ET))
    to_rows(scale, col_scale)
    scale_rows(phT, col_scale, scaled_p)
    products(E, scaled_p, F2)
    to_rows(grad_scale / row_total(2), row_scale)
    scale_rows(sh, row_scale, scaled_s)

    def chunk(index):
        rows = rows_at(index * OWN, OWN, OWN)
        product = jnp.dot(ET[rows, :], scaled_s[...], preferred_element_type=F32)
        return P1[rows, :] - wide(col_scale[rows, :]) * product

    def ahead(d):
        return lax.rem(z + d, Z)

    def part(values, j):
        return values[j * SUB : (j + 1) * SUB, :]

    def rs_r(d, j):
        return remote(snd_r.at[d - 1, j], rcv_r.at[d - 1, j], rsr_s.at[d - 1, j], rsr_r.at[d - 1, j], right)

    def rs_l(d, j):
        return remote(snd_l.at[d - 1, j], rcv_l.at[d - 1, j], rsl_s.at[d - 1, j], rsl_r.at[d - 1, j], left)

    values = chunk(ahead(4))
    for j in (0, 1):
        snd_r[3, j] = part(values, j)
        rs_r(4, j).start()
    for j in (2, 3):
        snd_l[3, j] = part(values, j)
        rs_l(4, j).start()
    values = chunk(ahead(3))
    for j in (2, 3):
        snd_r[2, j] = part(values, j)
        rs_r(3, j).start()
    for j in (0, 1):
        snd_r[2, j] = part(values, j)
    values = chunk(ahead(Z - 3))
    for j in (0, 1):
        snd_l[2, j] = part(values, j)
        rs_l(3, j).start()
    for j in (2, 3):
        snd_l[2, j] = part(values, j)

    F1[...] = F1[...] * wide(a_scale[...]) - F2[...] * wide(row_scale[...])
    feature_pair = remote(F1.at[rows_at((1 - core) * HALF, HALF, HALF)], f_sib, fc_s, fc_r, sibling)
    feature_pair.start()

    def pass_on(d, j_right, j_left):
        for j in j_right:
            rs_r(d + 1, j).wait_recv()
            snd_r[d - 1, j] = snd_r[d - 1, j] + rcv_r[d, j]
            rs_r(d, j).start()
        for j in j_left:
            rs_l(d + 1, j).wait_recv()
            snd_l[d - 1, j] = snd_l[d - 1, j] + rcv_l[d, j]
            rs_l(d, j).start()

    def own_terms(d):
        values = chunk(ahead(d))
        for j in range(4):
            snd_r[d - 1, j] = part(values, j)
        values = chunk(ahead(Z - d))
        for j in range(4):
            snd_l[d - 1, j] = part(values, j)

    own_terms(2)
    pass_on(3, (0, 1), (2, 3))
    own_terms(1)
    values = chunk(z)
    for j in range(4):
        own[j] = part(values, j)

    feature_pair.wait_recv()
    mine = rows_at(core * HALF, HALF, HALF)
    F2[mine, :] = F1[mine, :] + f_sib[...]

    def piece(c):
        return rows_at(core * HALF + c * PIECE, PIECE, PIECE)

    def piece_copy(d):
        return remote(
            F2.at[piece(lax.rem(chip + d, CHIPS))], f_recv.at[d - 1], fx_s.at[d - 1], fx_r.at[d - 1],
            same_core(d),
        )

    for d in range(1, 5):
        piece_copy(d).start()
    pass_on(2, (2, 3), (0, 1))
    for d in range(5, 12):
        piece_copy(d).start()
    pass_on(2, (0, 1), (2, 3))
    for d in range(12, CHIPS):
        piece_copy(d).start()
    pass_on(1, (2, 3), (0, 1))
    for i in range(3):
        for d in range(1, Z):
            col_copy(i, d).wait_send()
    pass_on(1, (0, 1), (2, 3))
    for i in range(4):
        pair_copy(i).wait_send()
        for d in range(1, CHIPS):
            chip_copy(i, d).wait_send()

    def ag_r(d, j):
        block = pg.at[rows_at(lax.rem(z + Z - (d - 1), Z) * OWN + j * SUB, SUB, SUB)]
        return remote(block, block, agr_s.at[d - 1, j], agr_r.at[d - 1, j], right)

    def ag_l(d, j):
        block = pg.at[rows_at(lax.rem(z + (d - 1), Z) * OWN + j * SUB, SUB, SUB)]
        return remote(block, block, agl_s.at[d - 1, j], agl_r.at[d - 1, j], left)

    def finish(j):
        rows = rows_at(z * OWN + j * SUB, SUB, SUB)
        terms = own[j] + rcv_r[0, j] + rcv_l[0, j]
        length = wide(own_len[j * SUB : (j + 1) * SUB, :])
        unit = own_unit[j * SUB : (j + 1) * SUB, :]
        pg[rows, :] = (terms - unit * jnp.sum(unit * terms, axis=1, keepdims=True)) / length
        ag_r(1, j).start()
        ag_l(1, j).start()

    for j in (2, 3):
        rs_r(1, j).wait_recv()
    for j in (0, 1):
        rs_l(1, j).wait_recv()
    for j in (0, 1):
        rs_r(1, j).wait_recv()
        finish(j)
    for j in (2, 3):
        rs_l(1, j).wait_recv()
        finish(j)

    for d in range(1, CHIPS):
        piece_copy(d).wait_recv()
    my_piece = piece(chip)
    terms = F2[my_piece, :] + jnp.sum(f_recv[...], axis=0)
    floats = sf[my_piece, :].astype(F32)
    length = jnp.sqrt(jnp.sum(floats * floats, axis=1, keepdims=True) + epsilon)
    unit = floats / length
    fg[my_piece, :] = (terms - unit * jnp.sum(unit * terms, axis=1, keepdims=True)) / length

    def spread_copy(d):
        return remote(fg.at[my_piece], fg.at[my_piece], fa_s.at[d - 1], fa_r.at[d - 1], same_core(d))

    def arrived_copy(d):
        block = fg.at[piece(lax.rem(chip + CHIPS - d, CHIPS))]
        return remote(block, block, fa_s.at[d - 1], fa_r.at[d - 1], same_core(d))

    def hand_copy(d):
        block = fg.at[piece(lax.rem(chip + CHIPS - d, CHIPS))]
        return remote(block, block, ff_s.at[d], ff_r.at[d], sibling)

    def hand_arrived(d):
        start = (1 - core) * HALF + lax.rem(chip + CHIPS - d, CHIPS) * PIECE
        block = fg.at[rows_at(start, PIECE, PIECE)]
        return remote(block, block, ff_s.at[d], ff_r.at[d], sibling)

    for d in range(1, CHIPS):
        spread_copy(d).start()
    hand_copy(0).start()

    def arrived_r(d, j):
        block = pg.at[rows_at(lax.rem(z + Z - d, Z) * OWN + j * SUB, SUB, SUB)]
        return remote(block, block, agr_s.at[d - 1, j], agr_r.at[d - 1, j], right)

    def arrived_l(d, j):
        block = pg.at[rows_at(lax.rem(z + d, Z) * OWN + j * SUB, SUB, SUB)]
        return remote(block, block, agl_s.at[d - 1, j], agl_r.at[d - 1, j], left)

    feature_pair.wait_send()
    for d in (1, 2):
        for j in range(4):
            arrived_r(d, j).wait_recv()
            ag_r(d + 1, j).start()
            arrived_l(d, j).wait_recv()
            ag_l(d + 1, j).start()
        for i in (4, 3) if d == 1 else (2, 1):
            for j in range(4):
                if i < 4 or j in (0, 1):
                    rs_r(i, j).wait_send()
                if i < 4 or j in (2, 3):
                    rs_l(i, j).wait_send()
        if d == 1:
            for i in range(1, CHIPS):
                piece_copy(i).wait_send()
    for j in (0, 1):
        arrived_r(3, j).wait_recv()
        ag_r(4, j).start()
        arrived_l(3, j).wait_recv()
    for j in (2, 3):
        arrived_l(3, j).wait_recv()
        ag_l(4, j).start()
        arrived_r(3, j).wait_recv()

    for d in range(1, CHIPS):
        arrived_copy(d).wait_recv()
        hand_copy(d).start()
    for d in range(1, CHIPS):
        spread_copy(d).wait_send()

    for j in (0, 1):
        arrived_r(4, j).wait_recv()
    for j in (2, 3):
        arrived_l(4, j).wait_recv()

    for d in range(CHIPS):
        hand_arrived(d).wait_recv()

    for d in (4, 3, 2, 1):
        for j in range(4):
            if d < 4 or j in (0, 1):
                ag_r(d, j).wait_send()
            if d < 4 or j in (2, 3):
                ag_l(d, j).wait_send()
    for d in range(CHIPS):
        hand_copy(d).wait_send()


def write_out(features, protos, features_out, protos_out, sems):
    first = pltpu.make_async_copy(features, features_out, sems.at[0])
    second = pltpu.make_async_copy(protos, protos_out, sems.at[1])
    first.start()
    second.start()
    first.wait()
    second.wait()


def on_device(student_features, teacher_features, student_protos, teacher_protos):
    vmem = pltpu.VMEM
    dma = pltpu.SemaphoreType.DMA
    features, protos = pl.pallas_call(
        kernel,
        out_shape=(pltpu.VMEM((CROPS, D), F32), pltpu.VMEM((PROTOS, D), F32)),
        in_specs=[pl.BlockSpec(memory_space=pl.ANY)] * 4,
        out_specs=[pl.BlockSpec(memory_space=pltpu.VMEM)] * 2,
        scratch_shapes=[
            vmem((CROPS, D), BF16),
            vmem((CROPS, D), BF16),
            vmem((D, PROTOS), BF16),
            vmem((D, PROTOS), BF16),
            vmem((CROPS, PROTOS), BF16),
            vmem((PROTOS, CROPS), BF16),
            vmem((CROPS, PROTOS), BF16),
            vmem((PROTOS, CROPS), BF16),
            vmem((CROPS, D), BF16),
            vmem((CROPS, D), BF16),
            vmem((D, PROTOS), BF16),
            vmem((PROTOS, D), BF16),
            vmem((D, PROTOS), BF16),
            vmem((PROTOS, D), BF16),
            vmem((CROPS, D), BF16),
            vmem((PROTOS, D), BF16),
            vmem((CROPS, 128), F32),
            vmem((PROTOS, 128), F32),
            vmem((CROPS, 128), F32),
            vmem((CROPS, D), F32),
            vmem((CROPS, D), F32),
            vmem((PROTOS, D), F32),
            vmem((3, 1, PROTOS), F32),
            vmem((3, Z - 1, 1, PROTOS), F32),
            vmem((4, 1, CROPS), F32),
            vmem((4, 1, CROPS), F32),
            vmem((4, 1, CROPS), F32),
            vmem((4, CHIPS - 1, 1, CROPS), F32),
            vmem((4, SUB, D), F32),
            vmem((4, 4, SUB, D), F32),
            vmem((4, 4, SUB, D), F32),
            vmem((4, 4, SUB, D), F32),
            vmem((4, 4, SUB, D), F32),
            vmem((OWN, D), F32),
            vmem((OWN, 128), F32),
            vmem((HALF, D), F32),
            vmem((CHIPS - 1, PIECE, D), F32),
            dma((4,)),
            dma((3, Z - 1)),
            dma((3, Z - 1)),
            dma((4,)),
            dma((4,)),
            dma((4, CHIPS - 1)),
            dma((4, CHIPS - 1)),
        ]
        + [dma((4, 4))] * 8
        + [
            dma,
            dma,
            dma((CHIPS - 1,)),
            dma((CHIPS - 1,)),
            dma((CHIPS - 1,)),
            dma((CHIPS - 1,)),
            dma((CHIPS,)),
            dma((CHIPS,)),
        ],
        compiler_params=pltpu.CompilerParams(
            collective_id=0, has_side_effects=True, vmem_limit_bytes=52 * 2**20
        ),
    )(student_features, teacher_features, student_protos, teacher_protos)
    return pl.pallas_call(
        write_out,
        out_shape=(
            jax.ShapeDtypeStruct((CROPS, D), F32),
            jax.ShapeDtypeStruct((PROTOS, D), F32),
        ),
        in_specs=[pl.BlockSpec(memory_space=pltpu.VMEM)] * 2,
        out_specs=[pl.BlockSpec(memory_space=pl.ANY)] * 2,
        scratch_shapes=[dma((2,))],
        compiler_params=pltpu.CompilerParams(vmem_limit_bytes=2 * 2**20),
    )(
        pltpu.with_memory_space_constraint(features, pltpu.VMEM),
        pltpu.with_memory_space_constraint(protos, pltpu.VMEM),
    )


def solution(mesh):
    return jax.shard_map(
        on_device,
        mesh=mesh,
        in_specs=(P("batch", None), P("batch", None), P(None, "proto"), P(None, "proto")),
        out_specs=(P("batch", None), P("proto", None)),
        check_vma=False,
    )
```

```python
import jax
import jax.numpy as jnp
from jax import lax
from jax.experimental import pallas as pl
from jax.experimental.pallas import tpu as pltpu
from jax.sharding import PartitionSpec as P

MESH = pl.DeviceIdType.MESH
F32 = jnp.float32
BF16 = jnp.bfloat16

epsilon = 1e-06
log2_e = 1.4426950408889634
teacher_rate = 25.0 * log2_e
student_rate = 10.0 * log2_e
grad_scale = 40960.0

CROPS = 1536
PROTOS = 2048
D = 256
Z = 8
CHIPS = 16
OWN = PROTOS // Z
SUBS = 4
SUB = OWN // SUBS
FIRST = tuple(range(SUBS // 2))
LAST = tuple(range(SUBS // 2, SUBS))
HALF = CROPS // 2
PIECE = HALF // CHIPS


def hops(offset):
    return min(offset[0], 4 - offset[0]) + min(offset[1], 4 - offset[1])


PLANE = sorted(
    [(y, x) for y in range(4) for x in range(4) if y + x > 0],
    key=lambda offset: (-hops(offset), offset),
)


def rows_at(start, size, step):
    return pl.ds(pl.multiple_of(start, step), size)


def normalise_rows(src, dst):
    def body(i, carry):
        rows = rows_at(i * 256, 256, 256)
        floats = src[rows, :].astype(F32)
        length = jnp.sqrt(jnp.sum(floats * floats, axis=1, keepdims=True) + epsilon)
        dst[rows, :] = (floats / length).astype(BF16)
        return carry

    lax.fori_loop(0, CROPS // 256, body, 0)


def normalise_columns(src, dst):
    def body(i, carry):
        cols = rows_at(i * 256, 256, 256)
        floats = src[:, cols].astype(F32)
        length = jnp.sqrt(jnp.sum(floats * floats, axis=0, keepdims=True) + epsilon)
        dst[:, cols] = (floats / length).astype(BF16)
        return carry

    lax.fori_loop(0, PROTOS // 256, body, 0)


def transpose_into(src, dst):
    def body(i, carry):
        cols = rows_at(i * 256, 256, 256)
        dst[cols, :] = src[:, cols].astype(F32).T.astype(BF16)
        return carry

    lax.fori_loop(0, PROTOS // 256, body, 0)


def exp_tiles(rows_ref, cols_ref, out, rate, transposed):
    count, width = out.shape
    block = count // 2
    dims = (((1,), (1,)), ((), ())) if transposed else (((1,), (0,)), ((), ()))

    def body(i, total):
        rows = rows_at(i * block, block, block)
        logits = lax.dot_general(rows_ref[rows, :], cols_ref[...], dims, preferred_element_type=F32)
        values = jnp.exp2(logits * rate)
        out[rows, :] = values.astype(BF16)
        return total + jnp.sum(values.reshape(block // 8, 8, width), axis=0)

    total = lax.fori_loop(0, 2, body, jnp.zeros((8, width), F32))
    return jnp.sum(total, axis=0, keepdims=True)


def vector_times(vector, matrix):
    high = vector.astype(BF16).astype(F32)
    low = vector - high
    row = lax.broadcasted_iota(jnp.int32, (16, vector.shape[1]), 0)
    left = jnp.where(row == 0, high, jnp.where(row == 1, low, 0.0)).astype(BF16)
    return jnp.sum(jnp.dot(left, matrix[...], preferred_element_type=F32), axis=0, keepdims=True)


def to_rows(vector, dst):
    for i in range(vector.shape[1] // 128):
        part = vector[:, i * 128 : (i + 1) * 128]
        dst[i * 128 : (i + 1) * 128, :] = jnp.broadcast_to(part, (128, 128)).T


def wide(narrow):
    return jnp.concatenate([narrow, narrow], axis=1)


def scale_rows(values, scale, dst):
    dst[...] = (values[...].astype(F32) * wide(scale[...])).astype(BF16)


def products(matrix, columns, dst):
    block = dst.shape[0] // 2

    def body(i, carry):
        rows = rows_at(i * block, block, block)
        dst[rows, :] = jnp.dot(matrix[rows, :], columns[...], preferred_element_type=F32)
        return carry

    lax.fori_loop(0, 2, body, 0)


def kernel(
    sf_in, tf_in, sp_in, tp_in, fg, pg, sf, tf, sp, tp,
    E, ET, S, ST, sh, th, ph, phT, ah, ahT,
    scaled_s, scaled_p, row_scale, col_scale, a_scale,
    F1, F2, P1,
    col_src, col_recv, row_part, row_sib, row_src, row_recv,
    own, snd_r, snd_l, rcv_r, rcv_l, own_unit, own_len,
    f_sib, f_recv, in_s,
    col_s, col_r, rc_s, rc_r, rp_s, rp_r,
    rsr_s, rsr_r, rsl_s, rsl_r, agr_s, agr_r, agl_s, agl_r,
    fc_s, fc_r, fx_s, fx_r, fa_s, fa_r, ff_s, ff_r,
):
    z = lax.axis_index("batch")
    p = lax.axis_index("proto")
    core = lax.rem(p, 2)
    chip = p // 2
    sibling = (z, chip * 2 + 1 - core)
    right = (lax.rem(z + 1, Z), p)
    left = (lax.rem(z + Z - 1, Z), p)

    def chip_at(d):
        y = lax.rem(chip // 4 + PLANE[d - 1][0], 4)
        x = lax.rem(chip + PLANE[d - 1][1], 4)
        return y * 4 + x

    def chip_from(d):
        y = lax.rem(chip // 4 + 4 - PLANE[d - 1][0], 4)
        x = lax.rem(chip + 4 - PLANE[d - 1][1], 4)
        return y * 4 + x

    def same_core(d):
        return (z, chip_at(d) * 2 + core)

    def load(i):
        src = (tf_in, tp_in, sf_in, sp_in)[i]
        dst = (tf, tp, sf, sp)[i]
        return pltpu.make_async_copy(src, dst, in_s.at[i])

    for i in range(4):
        load(i).start()

    barrier = pltpu.get_barrier_semaphore()

    def greet_z(d, carry):
        pl.semaphore_signal(barrier, inc=1, device_id=(lax.rem(z + d, Z), p), device_id_type=MESH)
        return carry

    lax.fori_loop(1, Z, greet_z, 0)

    def greet_plane(d, carry):
        target = (z, lax.rem(chip + d, CHIPS) * 2 + core)
        pl.semaphore_signal(barrier, inc=1, device_id=target, device_id_type=MESH)
        return carry

    lax.fori_loop(1, CHIPS, greet_plane, 0)
    pl.semaphore_signal(barrier, inc=1, device_id=sibling, device_id_type=MESH)

    def remote(src, dst, ss, rs, target):
        return pltpu.make_async_remote_copy(
            src_ref=src, dst_ref=dst, send_sem=ss, recv_sem=rs, device_id=target, device_id_type=MESH
        )

    def col_copy(i, d):
        return remote(
            col_src.at[i], col_recv.at[i, d - 1], col_s.at[i, d - 1], col_r.at[i, d - 1],
            (lax.rem(z + d, Z), p),
        )

    def col_send(i, partial):
        col_src[i] = partial
        for d in (4, 3, 5, 2, 6, 1, 7):
            col_copy(i, d).start()

    def col_total(i):
        for d in (1, 7, 2, 6, 3, 5, 4):
            col_copy(i, d).wait_recv()
        return col_src[i] + jnp.sum(col_recv[i], axis=0)

    def pair_copy(i):
        return remote(row_part.at[i], row_sib.at[i], rc_s.at[i], rc_r.at[i], sibling)

    def chip_copy(i, d):
        return remote(
            row_src.at[i], row_recv.at[i, d - 1], rp_s.at[i, d - 1], rp_r.at[i, d - 1], same_core(d)
        )

    def row_send(i, partial):
        row_part[i] = partial
        pair_copy(i).start()
        pair_copy(i).wait_recv()
        row_src[i] = row_part[i] + row_sib[i]
        for d in range(1, CHIPS):
            chip_copy(i, d).start()

    def row_total(i):
        for d in reversed(range(1, CHIPS)):
            chip_copy(i, d).wait_recv()
        return row_src[i] + jnp.sum(row_recv[i], axis=0)

    load(0).wait()
    normalise_rows(tf, th)
    load(1).wait()
    normalise_columns(tp, ah)
    partial = exp_tiles(th, ah, E, teacher_rate, False)
    pl.semaphore_wait(barrier, Z - 1 + CHIPS - 1 + 1)

    col_send(0, partial)
    transpose_into(ah, ahT)
    exp_tiles(ahT, th, ET, teacher_rate, True)
    scale = 1.0 / col_total(0)

    row_send(0, vector_times(scale, ET))
    load(2).wait()
    normalise_rows(sf, sh)
    load(3).wait()
    normalise_columns(sp, ph)
    transpose_into(ph, phT)
    floats = sp[:, rows_at(z * OWN, OWN, OWN)].astype(F32).T
    length = jnp.sqrt(jnp.sum(floats * floats, axis=1, keepdims=True) + epsilon)
    own_len[...] = jnp.broadcast_to(length, (OWN, 128))
    own_unit[...] = floats / length
    scale = 1.0 / row_total(0)

    col_send(1, vector_times(scale, E))
    student_partial = exp_tiles(phT, sh, ST, student_rate, True)
    exp_tiles(sh, ph, S, student_rate, False)
    scale = 1.0 / col_total(1)

    row_send(1, vector_times(scale, ET))
    row_send(3, student_partial)
    products(S, phT, F1)
    scale = 1.0 / row_total(1)

    col_send(2, vector_times(scale, E))
    to_rows(grad_scale / row_total(3), a_scale)
    scale_rows(sh, a_scale, scaled_s)
    products(ST, scaled_s, P1)
    scale = 1.0 / col_total(2)

    row_send(2, vector_times(scale, ET))
    to_rows(scale, col_scale)
    scale_rows(phT, col_scale, scaled_p)
    products(E, scaled_p, F2)
    to_rows(grad_scale / row_total(2), row_scale)
    scale_rows(sh, row_scale, scaled_s)

    def chunk(index):
        rows = rows_at(index * OWN, OWN, OWN)
        product = jnp.dot(ET[rows, :], scaled_s[...], preferred_element_type=F32)
        return P1[rows, :] - wide(col_scale[rows, :]) * product

    def ahead(d):
        return lax.rem(z + d, Z)

    def part(values, j):
        return values[j * SUB : (j + 1) * SUB, :]

    def rs_r(d, j):
        return remote(snd_r.at[d - 1, j], rcv_r.at[d - 1, j], rsr_s.at[d - 1, j], rsr_r.at[d - 1, j], right)

    def rs_l(d, j):
        return remote(snd_l.at[d - 1, j], rcv_l.at[d - 1, j], rsl_s.at[d - 1, j], rsl_r.at[d - 1, j], left)

    values = chunk(ahead(4))
    for j in FIRST:
        snd_r[3, j] = part(values, j)
        rs_r(4, j).start()
    for j in LAST:
        snd_l[3, j] = part(values, j)
        rs_l(4, j).start()
    values = chunk(ahead(3))
    for j in LAST:
        snd_r[2, j] = part(values, j)
        rs_r(3, j).start()
    for j in FIRST:
        snd_r[2, j] = part(values, j)
    values = chunk(ahead(Z - 3))
    for j in FIRST:
        snd_l[2, j] = part(values, j)
        rs_l(3, j).start()
    for j in LAST:
        snd_l[2, j] = part(values, j)

    F1[...] = F1[...] * wide(a_scale[...]) - F2[...] * wide(row_scale[...])
    feature_pair = remote(F1.at[rows_at((1 - core) * HALF, HALF, HALF)], f_sib, fc_s, fc_r, sibling)
    feature_pair.start()

    def pass_on(d, j_right, j_left):
        for i, j in zip(j_right, j_left):
            rs_r(d + 1, i).wait_recv()
            snd_r[d - 1, i] = snd_r[d - 1, i] + rcv_r[d, i]
            rs_r(d, i).start()
            rs_l(d + 1, j).wait_recv()
            snd_l[d - 1, j] = snd_l[d - 1, j] + rcv_l[d, j]
            rs_l(d, j).start()

    def own_terms(d):
        values = chunk(ahead(d))
        for j in range(SUBS):
            snd_r[d - 1, j] = part(values, j)
        values = chunk(ahead(Z - d))
        for j in range(SUBS):
            snd_l[d - 1, j] = part(values, j)

    own_terms(2)
    pass_on(3, FIRST, LAST)
    own_terms(1)
    values = chunk(z)
    for j in range(SUBS):
        own[j] = part(values, j)

    feature_pair.wait_recv()
    mine = rows_at(core * HALF, HALF, HALF)
    F2[mine, :] = F1[mine, :] + f_sib[...]

    def piece(c):
        return rows_at(core * HALF + c * PIECE, PIECE, PIECE)

    def piece_copy(d):
        return remote(
            F2.at[piece(chip_at(d))], f_recv.at[d - 1], fx_s.at[d - 1], fx_r.at[d - 1],
            same_core(d),
        )

    for d in range(1, 5):
        piece_copy(d).start()
    pass_on(2, LAST, FIRST)
    for d in range(5, 12):
        piece_copy(d).start()
    pass_on(2, FIRST, LAST)
    for d in range(12, CHIPS):
        piece_copy(d).start()
    pass_on(1, LAST, FIRST)
    for i in range(3):
        for d in range(1, Z):
            col_copy(i, d).wait_send()
    pass_on(1, FIRST, LAST)
    for i in range(4):
        pair_copy(i).wait_send()
        for d in range(1, CHIPS):
            chip_copy(i, d).wait_send()

    def ag_r(d, j):
        block = pg.at[rows_at(lax.rem(z + Z - (d - 1), Z) * OWN + j * SUB, SUB, SUB)]
        return remote(block, block, agr_s.at[d - 1, j], agr_r.at[d - 1, j], right)

    def ag_l(d, j):
        block = pg.at[rows_at(lax.rem(z + (d - 1), Z) * OWN + j * SUB, SUB, SUB)]
        return remote(block, block, agl_s.at[d - 1, j], agl_r.at[d - 1, j], left)

    def finish(j):
        rows = rows_at(z * OWN + j * SUB, SUB, SUB)
        terms = own[j] + rcv_r[0, j] + rcv_l[0, j]
        length = wide(own_len[j * SUB : (j + 1) * SUB, :])
        unit = own_unit[j * SUB : (j + 1) * SUB, :]
        pg[rows, :] = (terms - unit * jnp.sum(unit * terms, axis=1, keepdims=True)) / length
        ag_r(1, j).start()
        ag_l(1, j).start()

    for j in LAST:
        rs_r(1, j).wait_recv()
    for j in FIRST:
        rs_l(1, j).wait_recv()
    for i, j in zip(FIRST, LAST):
        rs_r(1, i).wait_recv()
        finish(i)
        rs_l(1, j).wait_recv()
        finish(j)

    for d in range(1, CHIPS):
        piece_copy(d).wait_recv()
    my_piece = piece(chip)
    terms = F2[my_piece, :] + jnp.sum(f_recv[...], axis=0)
    floats = sf[my_piece, :].astype(F32)
    length = jnp.sqrt(jnp.sum(floats * floats, axis=1, keepdims=True) + epsilon)
    unit = floats / length
    fg[my_piece, :] = (terms - unit * jnp.sum(unit * terms, axis=1, keepdims=True)) / length

    def spread_copy(d):
        return remote(fg.at[my_piece], fg.at[my_piece], fa_s.at[d - 1], fa_r.at[d - 1], same_core(d))

    def arrived_copy(d):
        block = fg.at[piece(chip_from(d))]
        return remote(block, block, fa_s.at[d - 1], fa_r.at[d - 1], same_core(d))

    def hand_copy(d):
        block = fg.at[piece(chip_from(d) if d else chip)]
        return remote(block, block, ff_s.at[d], ff_r.at[d], sibling)

    def hand_arrived(d):
        start = (1 - core) * HALF + (chip_from(d) if d else chip) * PIECE
        block = fg.at[rows_at(start, PIECE, PIECE)]
        return remote(block, block, ff_s.at[d], ff_r.at[d], sibling)

    for d in range(1, CHIPS):
        spread_copy(d).start()
    hand_copy(0).start()

    def arrived_r(d, j):
        block = pg.at[rows_at(lax.rem(z + Z - d, Z) * OWN + j * SUB, SUB, SUB)]
        return remote(block, block, agr_s.at[d - 1, j], agr_r.at[d - 1, j], right)

    def arrived_l(d, j):
        block = pg.at[rows_at(lax.rem(z + d, Z) * OWN + j * SUB, SUB, SUB)]
        return remote(block, block, agl_s.at[d - 1, j], agl_r.at[d - 1, j], left)

    feature_pair.wait_send()
    for d in (1, 2):
        for j in range(SUBS):
            arrived_r(d, j).wait_recv()
            ag_r(d + 1, j).start()
            arrived_l(d, j).wait_recv()
            ag_l(d + 1, j).start()
        for i in (4, 3) if d == 1 else (2, 1):
            for j in range(SUBS):
                if i < 4 or j in FIRST:
                    rs_r(i, j).wait_send()
                if i < 4 or j in LAST:
                    rs_l(i, j).wait_send()
        if d == 1:
            for i in range(1, CHIPS):
                piece_copy(i).wait_send()
    for j in FIRST:
        arrived_r(3, j).wait_recv()
        ag_r(4, j).start()
        arrived_l(3, j).wait_recv()
    for j in LAST:
        arrived_l(3, j).wait_recv()
        ag_l(4, j).start()
        arrived_r(3, j).wait_recv()

    for d in range(1, CHIPS):
        arrived_copy(d).wait_recv()
        hand_copy(d).start()
    for d in range(1, CHIPS):
        spread_copy(d).wait_send()

    for j in FIRST:
        arrived_r(4, j).wait_recv()
    for j in LAST:
        arrived_l(4, j).wait_recv()

    for d in range(CHIPS):
        hand_arrived(d).wait_recv()

    for d in (4, 3, 2, 1):
        for j in range(SUBS):
            if d < 4 or j in FIRST:
                ag_r(d, j).wait_send()
            if d < 4 or j in LAST:
                ag_l(d, j).wait_send()
    for d in range(CHIPS):
        hand_copy(d).wait_send()


def write_out(features, protos, features_out, protos_out, sems):
    copies = []
    for i in range(4):
        for src, dst in ((features, features_out), (protos, protos_out)):
            rows = pl.ds(i * (src.shape[0] // 4), src.shape[0] // 4)
            copies.append(pltpu.make_async_copy(src.at[rows], dst.at[rows], sems.at[len(copies)]))
    for copy in copies:
        copy.start()
    for copy in copies:
        copy.wait()


def on_device(student_features, teacher_features, student_protos, teacher_protos):
    vmem = pltpu.VMEM
    dma = pltpu.SemaphoreType.DMA
    features, protos = pl.pallas_call(
        kernel,
        out_shape=(pltpu.VMEM((CROPS, D), F32), pltpu.VMEM((PROTOS, D), F32)),
        in_specs=[pl.BlockSpec(memory_space=pl.ANY)] * 4,
        out_specs=[pl.BlockSpec(memory_space=pltpu.VMEM)] * 2,
        scratch_shapes=[
            vmem((CROPS, D), BF16),
            vmem((CROPS, D), BF16),
            vmem((D, PROTOS), BF16),
            vmem((D, PROTOS), BF16),
            vmem((CROPS, PROTOS), BF16),
            vmem((PROTOS, CROPS), BF16),
            vmem((CROPS, PROTOS), BF16),
            vmem((PROTOS, CROPS), BF16),
            vmem((CROPS, D), BF16),
            vmem((CROPS, D), BF16),
            vmem((D, PROTOS), BF16),
            vmem((PROTOS, D), BF16),
            vmem((D, PROTOS), BF16),
            vmem((PROTOS, D), BF16),
            vmem((CROPS, D), BF16),
            vmem((PROTOS, D), BF16),
            vmem((CROPS, 128), F32),
            vmem((PROTOS, 128), F32),
            vmem((CROPS, 128), F32),
            vmem((CROPS, D), F32),
            vmem((CROPS, D), F32),
            vmem((PROTOS, D), F32),
            vmem((3, 1, PROTOS), F32),
            vmem((3, Z - 1, 1, PROTOS), F32),
            vmem((4, 1, CROPS), F32),
            vmem((4, 1, CROPS), F32),
            vmem((4, 1, CROPS), F32),
            vmem((4, CHIPS - 1, 1, CROPS), F32),
            vmem((SUBS, SUB, D), F32),
            vmem((4, SUBS, SUB, D), F32),
            vmem((4, SUBS, SUB, D), F32),
            vmem((4, SUBS, SUB, D), F32),
            vmem((4, SUBS, SUB, D), F32),
            vmem((OWN, D), F32),
            vmem((OWN, 128), F32),
            vmem((HALF, D), F32),
            vmem((CHIPS - 1, PIECE, D), F32),
            dma((4,)),
            dma((3, Z - 1)),
            dma((3, Z - 1)),
            dma((4,)),
            dma((4,)),
            dma((4, CHIPS - 1)),
            dma((4, CHIPS - 1)),
        ]
        + [dma((4, SUBS))] * 8
        + [
            dma,
            dma,
            dma((CHIPS - 1,)),
            dma((CHIPS - 1,)),
            dma((CHIPS - 1,)),
            dma((CHIPS - 1,)),
            dma((CHIPS,)),
            dma((CHIPS,)),
        ],
        compiler_params=pltpu.CompilerParams(
            collective_id=0, has_side_effects=True, vmem_limit_bytes=52 * 2**20
        ),
    )(student_features, teacher_features, student_protos, teacher_protos)
    return pl.pallas_call(
        write_out,
        out_shape=(
            jax.ShapeDtypeStruct((CROPS, D), F32),
            jax.ShapeDtypeStruct((PROTOS, D), F32),
        ),
        in_specs=[pl.BlockSpec(memory_space=pltpu.VMEM)] * 2,
        out_specs=[pl.BlockSpec(memory_space=pl.ANY)] * 2,
        scratch_shapes=[dma((8,))],
        compiler_params=pltpu.CompilerParams(vmem_limit_bytes=2 * 2**20),
    )(
        pltpu.with_memory_space_constraint(features, pltpu.VMEM),
        pltpu.with_memory_space_constraint(protos, pltpu.VMEM),
    )


def solution(mesh):
    return jax.shard_map(
        on_device,
        mesh=mesh,
        in_specs=(P("batch", None), P("batch", None), P(None, "proto"), P(None, "proto")),
        out_specs=(P("batch", None), P("proto", None)),
        check_vma=False,
    )
```

```python
import jax
import jax.numpy as jnp
from jax import lax
from jax.experimental import pallas as pl
from jax.experimental.pallas import tpu as pltpu
from jax.sharding import PartitionSpec as P

MESH = pl.DeviceIdType.MESH
F32 = jnp.float32
BF16 = jnp.bfloat16

epsilon = 1e-06
log2_e = 1.4426950408889634
teacher_rate = 25.0 * log2_e
student_rate = 10.0 * log2_e
grad_scale = 40960.0

CROPS = 1536
PROTOS = 2048
D = 256
Z = 8
CHIPS = 16
OWN = PROTOS // Z
SUBS = 4
SUB = OWN // SUBS
FIRST = tuple(range(SUBS // 2))
LAST = tuple(range(SUBS // 2, SUBS))
HALF = CROPS // 2
PIECE = HALF // CHIPS


def hops(offset):
    return min(offset[0], 4 - offset[0]) + min(offset[1], 4 - offset[1])


PLANE = sorted(
    [(y, x) for y in range(4) for x in range(4) if y + x > 0],
    key=lambda offset: (-hops(offset), offset),
)


def rows_at(start, size, step):
    return pl.ds(pl.multiple_of(start, step), size)


def normalise_rows(src, dst):
    floats = src[...].astype(F32)
    length = jnp.sqrt(jnp.sum(floats * floats, axis=1, keepdims=True) + epsilon)
    dst[...] = (floats / length).astype(BF16)


def normalise_columns(src, dst):
    floats = src[...].astype(F32)
    length = jnp.sqrt(jnp.sum(floats * floats, axis=0, keepdims=True) + epsilon)
    dst[...] = (floats / length).astype(BF16)


def transpose_into(src, dst):
    def body(i, carry):
        cols = rows_at(i * 256, 256, 256)
        dst[cols, :] = src[:, cols].astype(F32).T.astype(BF16)
        return carry

    lax.fori_loop(0, PROTOS // 256, body, 0)


def exp_tiles(rows_ref, cols_ref, out, rate, transposed):
    count, width = out.shape
    block = count // 2
    dims = (((1,), (1,)), ((), ())) if transposed else (((1,), (0,)), ((), ()))

    def body(i, total):
        rows = rows_at(i * block, block, block)
        logits = lax.dot_general(rows_ref[rows, :], cols_ref[...], dims, preferred_element_type=F32)
        values = jnp.exp2(logits * rate)
        out[rows, :] = values.astype(BF16)
        return total + jnp.sum(values.reshape(block // 8, 8, width), axis=0)

    total = lax.fori_loop(0, 2, body, jnp.zeros((8, width), F32))
    return jnp.sum(total, axis=0, keepdims=True)


def vector_times(vector, matrix):
    high = vector.astype(BF16).astype(F32)
    low = vector - high
    row = lax.broadcasted_iota(jnp.int32, (16, vector.shape[1]), 0)
    left = jnp.where(row == 0, high, jnp.where(row == 1, low, 0.0)).astype(BF16)
    return jnp.sum(jnp.dot(left, matrix[...], preferred_element_type=F32), axis=0, keepdims=True)


def to_rows(vector, dst):
    for i in range(vector.shape[1] // 128):
        part = vector[:, i * 128 : (i + 1) * 128]
        dst[i * 128 : (i + 1) * 128, :] = jnp.broadcast_to(part, (128, 128)).T


def wide(narrow):
    return jnp.concatenate([narrow, narrow], axis=1)


def scale_rows(values, scale, dst):
    dst[...] = (values[...].astype(F32) * wide(scale[...])).astype(BF16)


def products(matrix, columns, dst):
    block = dst.shape[0] // 2

    def body(i, carry):
        rows = rows_at(i * block, block, block)
        dst[rows, :] = jnp.dot(matrix[rows, :], columns[...], preferred_element_type=F32)
        return carry

    lax.fori_loop(0, 2, body, 0)


def kernel(
    sf_in, tf_in, sp_in, tp_in, fg, pg, sf, tf, sp, tp,
    E, ET, S, ST, sh, th, ph, phT, ah, ahT,
    scaled_s, scaled_p, row_scale, col_scale, a_scale,
    F1, F2, P1,
    col_src, col_recv, row_part, row_sib, row_src, row_recv,
    own, snd_r, snd_l, rcv_r, rcv_l, own_unit, own_len,
    f_sib, f_recv, in_s,
    col_s, col_r, rc_s, rc_r, rp_s, rp_r,
    rsr_s, rsr_r, rsl_s, rsl_r, agr_s, agr_r, agl_s, agl_r,
    fc_s, fc_r, fx_s, fx_r, fa_s, fa_r, ff_s, ff_r,
):
    z = lax.axis_index("batch")
    p = lax.axis_index("proto")
    core = lax.rem(p, 2)
    chip = p // 2
    sibling = (z, chip * 2 + 1 - core)
    right = (lax.rem(z + 1, Z), p)
    left = (lax.rem(z + Z - 1, Z), p)

    def chip_at(d):
        y = lax.rem(chip // 4 + PLANE[d - 1][0], 4)
        x = lax.rem(chip + PLANE[d - 1][1], 4)
        return y * 4 + x

    def chip_from(d):
        y = lax.rem(chip // 4 + 4 - PLANE[d - 1][0], 4)
        x = lax.rem(chip + 4 - PLANE[d - 1][1], 4)
        return y * 4 + x

    def same_core(d):
        return (z, chip_at(d) * 2 + core)

    def load(i):
        src = (tf_in, tp_in, sf_in, sp_in)[i]
        dst = (tf, tp, sf, sp)[i]
        return pltpu.make_async_copy(src, dst, in_s.at[i])

    for i in range(4):
        load(i).start()

    barrier = pltpu.get_barrier_semaphore()

    def greet_z(d, carry):
        pl.semaphore_signal(barrier, inc=1, device_id=(lax.rem(z + d, Z), p), device_id_type=MESH)
        return carry

    lax.fori_loop(1, Z, greet_z, 0)

    def greet_plane(d, carry):
        target = (z, lax.rem(chip + d, CHIPS) * 2 + core)
        pl.semaphore_signal(barrier, inc=1, device_id=target, device_id_type=MESH)
        return carry

    lax.fori_loop(1, CHIPS, greet_plane, 0)
    pl.semaphore_signal(barrier, inc=1, device_id=sibling, device_id_type=MESH)

    def remote(src, dst, ss, rs, target):
        return pltpu.make_async_remote_copy(
            src_ref=src, dst_ref=dst, send_sem=ss, recv_sem=rs, device_id=target, device_id_type=MESH
        )

    def col_copy(i, d):
        return remote(
            col_src.at[i], col_recv.at[i, d - 1], col_s.at[i, d - 1], col_r.at[i, d - 1],
            (lax.rem(z + d, Z), p),
        )

    def col_send(i, partial):
        col_src[i] = partial
        for d in (4, 3, 5, 2, 6, 1, 7):
            col_copy(i, d).start()

    def col_total(i):
        for d in (1, 7, 2, 6, 3, 5, 4):
            col_copy(i, d).wait_recv()
        return col_src[i] + jnp.sum(col_recv[i], axis=0)

    def pair_copy(i):
        return remote(row_part.at[i], row_sib.at[i], rc_s.at[i], rc_r.at[i], sibling)

    def chip_copy(i, d):
        return remote(
            row_src.at[i], row_recv.at[i, d - 1], rp_s.at[i, d - 1], rp_r.at[i, d - 1], same_core(d)
        )

    def row_send(i, partial):
        row_part[i] = partial
        pair_copy(i).start()
        pair_copy(i).wait_recv()
        row_src[i] = row_part[i] + row_sib[i]
        for d in range(1, CHIPS):
            chip_copy(i, d).start()

    def row_total(i):
        for d in reversed(range(1, CHIPS)):
            chip_copy(i, d).wait_recv()
        return row_src[i] + jnp.sum(row_recv[i], axis=0)

    load(0).wait()
    normalise_rows(tf, th)
    load(1).wait()
    normalise_columns(tp, ah)
    partial = exp_tiles(th, ah, E, teacher_rate, False)
    pl.semaphore_wait(barrier, Z - 1 + CHIPS - 1 + 1)

    col_send(0, partial)
    transpose_into(ah, ahT)
    exp_tiles(ahT, th, ET, teacher_rate, True)
    scale = 1.0 / col_total(0)

    row_send(0, vector_times(scale, ET))
    load(2).wait()
    normalise_rows(sf, sh)
    load(3).wait()
    normalise_columns(sp, ph)
    transpose_into(ph, phT)
    floats = sp[:, rows_at(z * OWN, OWN, OWN)].astype(F32).T
    length = jnp.sqrt(jnp.sum(floats * floats, axis=1, keepdims=True) + epsilon)
    own_len[...] = jnp.broadcast_to(length, (OWN, 128))
    own_unit[...] = floats / length
    scale = 1.0 / row_total(0)

    col_send(1, vector_times(scale, E))
    student_partial = exp_tiles(phT, sh, ST, student_rate, True)
    exp_tiles(sh, ph, S, student_rate, False)
    scale = 1.0 / col_total(1)

    row_send(1, vector_times(scale, ET))
    row_send(3, student_partial)
    products(S, phT, F1)
    scale = 1.0 / row_total(1)

    col_send(2, vector_times(scale, E))
    to_rows(grad_scale / row_total(3), a_scale)
    scale_rows(sh, a_scale, scaled_s)
    products(ST, scaled_s, P1)
    scale = 1.0 / col_total(2)

    row_send(2, vector_times(scale, ET))
    to_rows(scale, col_scale)
    scale_rows(phT, col_scale, scaled_p)
    products(E, scaled_p, F2)
    vector = grad_scale / row_total(2)
    for i in range(CROPS // 128):
        rows = slice(i * 128, (i + 1) * 128)
        scale = jnp.broadcast_to(vector[:, rows], (128, 128)).T
        row_scale[rows, :] = scale
        scaled_s[rows, :] = (sh[rows, :].astype(F32) * wide(scale)).astype(BF16)

    def chunk(index):
        rows = rows_at(index * OWN, OWN, OWN)
        product = jnp.dot(ET[rows, :], scaled_s[...], preferred_element_type=F32)
        return P1[rows, :] - wide(col_scale[rows, :]) * product

    def ahead(d):
        return lax.rem(z + d, Z)

    def part(values, j):
        return values[j * SUB : (j + 1) * SUB, :]

    def rs_r(d, j):
        return remote(snd_r.at[d - 1, j], rcv_r.at[d - 1, j], rsr_s.at[d - 1, j], rsr_r.at[d - 1, j], right)

    def rs_l(d, j):
        return remote(snd_l.at[d - 1, j], rcv_l.at[d - 1, j], rsl_s.at[d - 1, j], rsl_r.at[d - 1, j], left)

    values = chunk(ahead(4))
    for j in FIRST:
        snd_r[3, j] = part(values, j)
        rs_r(4, j).start()
    for j in LAST:
        snd_l[3, j] = part(values, j)
        rs_l(4, j).start()
    values = chunk(ahead(3))
    for j in LAST:
        snd_r[2, j] = part(values, j)
        rs_r(3, j).start()
    for j in FIRST:
        snd_r[2, j] = part(values, j)
    values = chunk(ahead(Z - 3))
    for j in FIRST:
        snd_l[2, j] = part(values, j)
        rs_l(3, j).start()
    for j in LAST:
        snd_l[2, j] = part(values, j)

    F1[...] = F1[...] * wide(a_scale[...]) - F2[...] * wide(row_scale[...])
    feature_pair = remote(F1.at[rows_at((1 - core) * HALF, HALF, HALF)], f_sib, fc_s, fc_r, sibling)
    feature_pair.start()

    def pass_on(d, j_right, j_left):
        for i, j in zip(j_right, j_left):
            rs_r(d + 1, i).wait_recv()
            snd_r[d - 1, i] = snd_r[d - 1, i] + rcv_r[d, i]
            rs_r(d, i).start()
            rs_l(d + 1, j).wait_recv()
            snd_l[d - 1, j] = snd_l[d - 1, j] + rcv_l[d, j]
            rs_l(d, j).start()

    def own_terms(d):
        values = chunk(ahead(d))
        for j in range(SUBS):
            snd_r[d - 1, j] = part(values, j)
        values = chunk(ahead(Z - d))
        for j in range(SUBS):
            snd_l[d - 1, j] = part(values, j)

    own_terms(2)
    pass_on(3, FIRST, LAST)
    own_terms(1)
    values = chunk(z)
    for j in range(SUBS):
        own[j] = part(values, j)

    feature_pair.wait_recv()
    mine = rows_at(core * HALF, HALF, HALF)
    F2[mine, :] = F1[mine, :] + f_sib[...]

    def piece(c):
        return rows_at(core * HALF + c * PIECE, PIECE, PIECE)

    def piece_copy(d):
        return remote(
            F2.at[piece(chip_at(d))], f_recv.at[d - 1], fx_s.at[d - 1], fx_r.at[d - 1],
            same_core(d),
        )

    for d in range(1, 5):
        piece_copy(d).start()
    pass_on(2, LAST, FIRST)
    for d in range(5, 12):
        piece_copy(d).start()
    pass_on(2, FIRST, LAST)
    for d in range(12, CHIPS):
        piece_copy(d).start()
    pass_on(1, LAST, FIRST)
    for i in range(3):
        for d in range(1, Z):
            col_copy(i, d).wait_send()
    pass_on(1, FIRST, LAST)
    for i in range(4):
        pair_copy(i).wait_send()
        for d in range(1, CHIPS):
            chip_copy(i, d).wait_send()

    def ag_r(d, j):
        block = pg.at[rows_at(lax.rem(z + Z - (d - 1), Z) * OWN + j * SUB, SUB, SUB)]
        return remote(block, block, agr_s.at[d - 1, j], agr_r.at[d - 1, j], right)

    def ag_l(d, j):
        block = pg.at[rows_at(lax.rem(z + (d - 1), Z) * OWN + j * SUB, SUB, SUB)]
        return remote(block, block, agl_s.at[d - 1, j], agl_r.at[d - 1, j], left)

    def finish(j):
        rows = rows_at(z * OWN + j * SUB, SUB, SUB)
        terms = own[j] + rcv_r[0, j] + rcv_l[0, j]
        length = wide(own_len[j * SUB : (j + 1) * SUB, :])
        unit = own_unit[j * SUB : (j + 1) * SUB, :]
        pg[rows, :] = (terms - unit * jnp.sum(unit * terms, axis=1, keepdims=True)) / length
        ag_r(1, j).start()
        ag_l(1, j).start()

    for j in LAST:
        rs_r(1, j).wait_recv()
    for j in FIRST:
        rs_l(1, j).wait_recv()
    for i, j in zip(FIRST, LAST):
        rs_r(1, i).wait_recv()
        finish(i)
        rs_l(1, j).wait_recv()
        finish(j)

    for d in range(1, CHIPS):
        piece_copy(d).wait_recv()
    my_piece = piece(chip)
    terms = F2[my_piece, :] + jnp.sum(f_recv[...], axis=0)
    floats = sf[my_piece, :].astype(F32)
    length = jnp.sqrt(jnp.sum(floats * floats, axis=1, keepdims=True) + epsilon)
    unit = floats / length
    fg[my_piece, :] = (terms - unit * jnp.sum(unit * terms, axis=1, keepdims=True)) / length

    def spread_copy(d):
        return remote(fg.at[my_piece], fg.at[my_piece], fa_s.at[d - 1], fa_r.at[d - 1], same_core(d))

    def arrived_copy(d):
        block = fg.at[piece(chip_from(d))]
        return remote(block, block, fa_s.at[d - 1], fa_r.at[d - 1], same_core(d))

    def hand_copy(d):
        block = fg.at[piece(chip_from(d) if d else chip)]
        return remote(block, block, ff_s.at[d], ff_r.at[d], sibling)

    def hand_arrived(d):
        start = (1 - core) * HALF + (chip_from(d) if d else chip) * PIECE
        block = fg.at[rows_at(start, PIECE, PIECE)]
        return remote(block, block, ff_s.at[d], ff_r.at[d], sibling)

    for d in range(1, CHIPS):
        spread_copy(d).start()
    hand_copy(0).start()

    def arrived_r(d, j):
        block = pg.at[rows_at(lax.rem(z + Z - d, Z) * OWN + j * SUB, SUB, SUB)]
        return remote(block, block, agr_s.at[d - 1, j], agr_r.at[d - 1, j], right)

    def arrived_l(d, j):
        block = pg.at[rows_at(lax.rem(z + d, Z) * OWN + j * SUB, SUB, SUB)]
        return remote(block, block, agl_s.at[d - 1, j], agl_r.at[d - 1, j], left)

    feature_pair.wait_send()
    for d in (1, 2):
        for j in range(SUBS):
            arrived_r(d, j).wait_recv()
            ag_r(d + 1, j).start()
            arrived_l(d, j).wait_recv()
            ag_l(d + 1, j).start()
        for i in (4, 3) if d == 1 else (2, 1):
            for j in range(SUBS):
                if i < 4 or j in FIRST:
                    rs_r(i, j).wait_send()
                if i < 4 or j in LAST:
                    rs_l(i, j).wait_send()
        if d == 1:
            for i in range(1, CHIPS):
                piece_copy(i).wait_send()
    for j in FIRST:
        arrived_r(3, j).wait_recv()
        ag_r(4, j).start()
        arrived_l(3, j).wait_recv()
    for j in LAST:
        arrived_l(3, j).wait_recv()
        ag_l(4, j).start()
        arrived_r(3, j).wait_recv()

    for d in range(1, CHIPS):
        arrived_copy(d).wait_recv()
        hand_copy(d).start()
    for d in range(1, CHIPS):
        spread_copy(d).wait_send()

    for j in FIRST:
        arrived_r(4, j).wait_recv()
    for j in LAST:
        arrived_l(4, j).wait_recv()

    for d in range(CHIPS):
        hand_arrived(d).wait_recv()

    for d in (4, 3, 2, 1):
        for j in range(SUBS):
            if d < 4 or j in FIRST:
                ag_r(d, j).wait_send()
            if d < 4 or j in LAST:
                ag_l(d, j).wait_send()
    for d in range(CHIPS):
        hand_copy(d).wait_send()


def write_out(features, protos, features_out, protos_out, sems):
    copies = []
    for i in range(4):
        for src, dst in ((features, features_out), (protos, protos_out)):
            rows = pl.ds(i * (src.shape[0] // 4), src.shape[0] // 4)
            copies.append(pltpu.make_async_copy(src.at[rows], dst.at[rows], sems.at[len(copies)]))
    for copy in copies:
        copy.start()
    for copy in copies:
        copy.wait()


def on_device(student_features, teacher_features, student_protos, teacher_protos):
    vmem = pltpu.VMEM
    dma = pltpu.SemaphoreType.DMA
    features, protos = pl.pallas_call(
        kernel,
        out_shape=(pltpu.VMEM((CROPS, D), F32), pltpu.VMEM((PROTOS, D), F32)),
        in_specs=[pl.BlockSpec(memory_space=pl.ANY)] * 4,
        out_specs=[pl.BlockSpec(memory_space=pltpu.VMEM)] * 2,
        scratch_shapes=[
            vmem((CROPS, D), BF16),
            vmem((CROPS, D), BF16),
            vmem((D, PROTOS), BF16),
            vmem((D, PROTOS), BF16),
            vmem((CROPS, PROTOS), BF16),
            vmem((PROTOS, CROPS), BF16),
            vmem((CROPS, PROTOS), BF16),
            vmem((PROTOS, CROPS), BF16),
            vmem((CROPS, D), BF16),
            vmem((CROPS, D), BF16),
            vmem((D, PROTOS), BF16),
            vmem((PROTOS, D), BF16),
            vmem((D, PROTOS), BF16),
            vmem((PROTOS, D), BF16),
            vmem((CROPS, D), BF16),
            vmem((PROTOS, D), BF16),
            vmem((CROPS, 128), F32),
            vmem((PROTOS, 128), F32),
            vmem((CROPS, 128), F32),
            vmem((CROPS, D), F32),
            vmem((CROPS, D), F32),
            vmem((PROTOS, D), F32),
            vmem((3, 1, PROTOS), F32),
            vmem((3, Z - 1, 1, PROTOS), F32),
            vmem((4, 1, CROPS), F32),
            vmem((4, 1, CROPS), F32),
            vmem((4, 1, CROPS), F32),
            vmem((4, CHIPS - 1, 1, CROPS), F32),
            vmem((SUBS, SUB, D), F32),
            vmem((4, SUBS, SUB, D), F32),
            vmem((4, SUBS, SUB, D), F32),
            vmem((4, SUBS, SUB, D), F32),
            vmem((4, SUBS, SUB, D), F32),
            vmem((OWN, D), F32),
            vmem((OWN, 128), F32),
            vmem((HALF, D), F32),
            vmem((CHIPS - 1, PIECE, D), F32),
            dma((4,)),
            dma((3, Z - 1)),
            dma((3, Z - 1)),
            dma((4,)),
            dma((4,)),
            dma((4, CHIPS - 1)),
            dma((4, CHIPS - 1)),
        ]
        + [dma((4, SUBS))] * 8
        + [
            dma,
            dma,
            dma((CHIPS - 1,)),
            dma((CHIPS - 1,)),
            dma((CHIPS - 1,)),
            dma((CHIPS - 1,)),
            dma((CHIPS,)),
            dma((CHIPS,)),
        ],
        compiler_params=pltpu.CompilerParams(
            collective_id=0, has_side_effects=True, vmem_limit_bytes=52 * 2**20
        ),
    )(student_features, teacher_features, student_protos, teacher_protos)
    return pl.pallas_call(
        write_out,
        out_shape=(
            jax.ShapeDtypeStruct((CROPS, D), F32),
            jax.ShapeDtypeStruct((PROTOS, D), F32),
        ),
        in_specs=[pl.BlockSpec(memory_space=pltpu.VMEM)] * 2,
        out_specs=[pl.BlockSpec(memory_space=pl.ANY)] * 2,
        scratch_shapes=[dma((8,))],
        compiler_params=pltpu.CompilerParams(vmem_limit_bytes=2 * 2**20),
    )(
        pltpu.with_memory_space_constraint(features, pltpu.VMEM),
        pltpu.with_memory_space_constraint(protos, pltpu.VMEM),
    )


def solution(mesh):
    return jax.shard_map(
        on_device,
        mesh=mesh,
        in_specs=(P("batch", None), P("batch", None), P(None, "proto"), P(None, "proto")),
        out_specs=(P("batch", None), P("proto", None)),
        check_vma=False,
    )
```
